32 devices in a mesh: freq: 4 (over z), tile: 8 (over y, x, core).
Axes of the slice: x: 2, y: 2, z: 4, core: 2. Of those that a mesh axis runs over, the one named last changes fastest.
Arguments:
- model_freq: bfloat16 [8, 16384, 384], P('freq', 'tile'), may hold values from -6 to 6
- recorded: bfloat16 [8, 16384, 384], P('freq', 'tile'), may hold values from -6 to 6
- v_factor: bfloat16 [8, 32, 32, 2, 64, 512], P('freq', 'tile'), may hold values from -0.25 to 0.25
- u_factor: bfloat16 [8, 32, 32, 2, 64, 512], P('freq', 'tile'), may hold values from -0.125 to 0.125
- tile_rank: int32 [8, 32, 32], P('freq', 'tile'), may hold values from 16 to 64
- tile_rows: int32 [32, 32], P('tile'), may hold values from 0 to 31, each once within a row
- omega: float32 [8], P('freq'), may hold values from 0.3 to 2.9
Outputs:
- lag_gradient: float32 [8, 16384, 192], P('freq', 'tile')
The draws below stay inside these ranges and needn't reach their ends.
Inputs may be any that keep to these rules, and one draw needn't show every extreme that they name: Each row of tile_rows is a permutation of 0 to 31.
All inputs are finite; a program needn't handle non-finite values.
Results may differ from the reference program's by a relative error of at most 0.0037.
Values may be sent and summed in bfloat16 or wider, within the bound.
A program may use at most 256 MiB of HBM per device.

```python
import jax
import jax.numpy as jnp
from jax import lax

TB = 32
TS = 512
RANK = 64
SOURCES = 192
ORDER = 16384
FREQS = 8
LAGS = 8


def touch_ends(drawn, key, low, high):
    spot = [jax.random.randint(jax.random.fold_in(key, axis), (), 0, length) for axis, length in enumerate(drawn.shape)]
    longest = drawn.shape.index(max(drawn.shape))
    beside = spot[:longest] + [(spot[longest] + 1) % drawn.shape[longest]] + spot[longest + 1:]
    return drawn.at[tuple(spot)].set(low).at[tuple(beside)].set(high)


def block_scale(key, shape, cuts, low, high):
    level = 1.0
    for position, parts in cuts:
        heights = jax.random.uniform(jax.random.fold_in(jax.random.fold_in(key, 6), position), (parts,), jnp.float32, low / len(cuts), high / len(cuts))
        level = level * jnp.repeat(jnp.exp(heights), shape[position] // parts).reshape((-1,) + (1,) * (len(shape) - 1 - position))
    return level


def bell_draw(rng, shape, scale, reach, shards=(), kind=jnp.bfloat16):
    result = scale * jax.random.normal(rng, shape, jnp.float32)
    if shards:
        result = result * block_scale(rng, shape, shards, -0.22, 0.18)
    return jnp.clip(result, -reach, reach).astype(kind)


def setup_inputs(seed: int = 0) -> dict:
    keys = jax.random.split(jax.random.key(seed), 8)
    model_freq = bell_draw(keys[0], (FREQS, ORDER, 2 * SOURCES), 1.0, 6.0, ((0, 4), (1, 8)))
    recorded = bell_draw(keys[1], (FREQS, ORDER, 2 * SOURCES), 1.0, 6.0, ((0, 4), (1, 8)))
    v_factor = bell_draw(keys[2], (FREQS, TB, TB, 2, RANK, TS), TS ** -0.5, 0.25, ((0, 4), (1, 8)))
    u_factor = bell_draw(keys[3], (FREQS, TB, TB, 2, RANK, TS), (TB * RANK) ** -0.5, 0.125, ((0, 4), (1, 8)))
    tile_rank = touch_ends(jax.random.randint(keys[4], (FREQS, TB, TB), RANK // 4, RANK + 1), jax.random.fold_in(keys[4], 1), RANK // 4, RANK).astype(jnp.int32)
    tile_rows = jax.vmap(lambda own: jax.random.permutation(own, TB))(jax.random.split(keys[5], TB)).reshape((TB, TB)).astype(jnp.int32)
    omega = jnp.clip(0.3 + 2.6000001 * jax.random.uniform(keys[6], (FREQS,), jnp.float32) ** block_scale(keys[6], (FREQS,), ((0, 4),), -0.2, 0.2), 0.3, 2.9)
    return {"model_freq": model_freq, "recorded": recorded, "v_factor": v_factor, "u_factor": u_factor, "tile_rank": tile_rank, "tile_rows": tile_rows, "omega": omega}


def reference(model_freq, recorded, v_factor, u_factor, tile_rank, tile_rows, omega):
    half = SOURCES
    select = (tile_rows[:, :, None] == jnp.arange(TB, dtype=jnp.int32)[None, None, :]).astype(jnp.float32)

    def one_freq(item):
        model_one, data_one, v_one, u_one, rank_one = item
        blocks = model_one.reshape(TB, TS, 2 * half).astype(jnp.float32)
        v_real = v_one[:, :, 0].astype(jnp.float32)
        v_imag = v_one[:, :, 1].astype(jnp.float32)
        first = jnp.einsum("jkrt,jts->jkrs", v_real, blocks)
        second = jnp.einsum("jkrt,jts->jkrs", v_imag, blocks)
        coeff = jnp.concatenate([first[..., :half] - second[..., half:], first[..., half:] + second[..., :half]], -1)
        keep = (jnp.arange(RANK, dtype=jnp.int32)[None, None, :] < rank_one[:, :, None]).astype(jnp.float32)[..., None]
        coeff = (coeff * keep).astype(jnp.bfloat16)
        natural = jnp.einsum("jki,jkrs->ijrs", select, coeff.astype(jnp.float32))
        u_real = u_one[:, :, 0].astype(jnp.float32)
        u_imag = u_one[:, :, 1].astype(jnp.float32)
        upper = jnp.einsum("ijrt,ijrs->its", u_real, natural)
        lower = jnp.einsum("ijrt,ijrs->its", u_imag, natural)
        forward = jnp.concatenate([upper[..., :half] - lower[..., half:], upper[..., half:] + lower[..., :half]], -1)
        resid = (forward - data_one.reshape(TB, TS, 2 * half).astype(jnp.float32)).astype(jnp.bfloat16)
        resid = resid.astype(jnp.float32)
        back_re = jnp.einsum("ijrt,its->ijrs", u_real, resid)
        back_im = jnp.einsum("ijrt,its->ijrs", u_imag, resid)
        back = jnp.concatenate([back_re[..., :half] + back_im[..., half:], back_re[..., half:] - back_im[..., :half]], -1)
        back = back.astype(jnp.bfloat16)
        slotted = jnp.einsum("jki,ijrs->jkrs", select, back.astype(jnp.float32)) * keep
        grad_a = jnp.einsum("jkrt,jkrs->jts", v_real, slotted)
        grad_b = jnp.einsum("jkrt,jkrs->jts", v_imag, slotted)
        grad = jnp.concatenate([grad_a[..., :half] + grad_b[..., half:], grad_a[..., half:] - grad_b[..., :half]], -1)
        return grad.reshape(TB * TS, 2 * half)

    grads = lax.map(one_freq, (model_freq, recorded, v_factor, u_factor, tile_rank))
    lag_axis = jnp.arange(LAGS, dtype=jnp.float32)
    phase = lag_axis[:, None] * omega[None, :]
    cosine = jnp.cos(phase)
    sine = jnp.sin(phase)
    total = jnp.einsum("lf,fns->lns", cosine, grads[..., :half], precision=lax.Precision.HIGHEST)
    total = total - jnp.einsum("lf,fns->lns", sine, grads[..., half:], precision=lax.Precision.HIGHEST)
    return total * (2.0 / FREQS)
```

```python
import functools

import jax
import jax.numpy as jnp
from jax import lax
from jax.experimental import pallas as pl
from jax.experimental.pallas import tpu as pltpu
from jax.sharding import PartitionSpec as P

VMEM_BYTES = 44 * 1024 * 1024
GROUP = 8


def turn(block):
    half = block.shape[-1] // 2
    return jnp.concatenate([-block[:, half:], block[:, :half]], -1)


def turn_back(block):
    half = block.shape[-1] // 2
    return jnp.concatenate([block[:, half:], -block[:, :half]], -1)


def dot(left, right):
    return lax.dot_general(left, right, (((1,), (0,)), ((), ())), preferred_element_type=jnp.float32)


def dot_rows(left, right):
    return lax.dot_general(left, right, (((0,), (0,)), ((), ())), preferred_element_type=jnp.float32)


def part_of(ref, lead, start, count, part):
    rank, width = ref.shape[-2], ref.shape[-1]
    return ref[(*lead, pl.ds(start, count), part)].reshape(count * rank, width)


def coeff_body(freq, rows_ref, rank_ref, v_ref, x_ref, out_ref, x2_ref):
    block = pl.program_id(0)
    tiles, rank, cols = v_ref.shape[2], v_ref.shape[4], x_ref.shape[-1]
    group = min(GROUP, tiles)
    x2_ref[...] = turn(x_ref[0, 0])
    row = lax.broadcasted_iota(jnp.int32, (rank, cols), 0)

    @pl.loop(0, tiles // group)
    def _(step):
        first = step * group
        total = dot(part_of(v_ref, (0, 0), first, group, 0), x_ref[0, 0])
        total += dot(part_of(v_ref, (0, 0), first, group, 1), x2_ref[...])
        for t in range(group):
            slot = first + t
            kept = row < rank_ref[freq, block, slot]
            tile = jnp.where(kept, total[t * rank : (t + 1) * rank], 0.0)
            out_ref[rows_ref[block, slot], 0] = tile.astype(out_ref.dtype)


def coeff_call(freq, tile_rows, tile_rank, v_factor, blocks):
    _, own, tiles, _, rank, width = v_factor.shape
    cols = blocks.shape[-1]
    return pl.pallas_call(
        functools.partial(coeff_body, freq),
        grid_spec=pltpu.PrefetchScalarGridSpec(
            num_scalar_prefetch=2,
            grid=(own,),
            in_specs=[
                pl.BlockSpec((1, 1, tiles, 2, rank, width), lambda j, *_: (freq, j, 0, 0, 0, 0)),
                pl.BlockSpec((1, 1, width, cols), lambda j, *_: (freq, j, 0, 0)),
            ],
            out_specs=pl.BlockSpec((tiles, 1, rank, cols), lambda j, *_: (0, j, 0, 0)),
            scratch_shapes=[pltpu.VMEM((width, cols), jnp.bfloat16)],
        ),
        out_shape=jax.ShapeDtypeStruct((tiles, own, rank, cols), jnp.bfloat16),
        compiler_params=pltpu.CompilerParams(vmem_limit_bytes=VMEM_BYTES),
        cost_estimate=pl.CostEstimate(
            flops=4 * own * tiles * rank * width * cols,
            bytes_accessed=own * tiles * rank * (4 * width + 2 * cols),
            transcendentals=0,
        ),
        name="coeff",
    )(tile_rows, tile_rank, v_factor, blocks)


def middle_body(u_ref, c_ref, seen_ref, *rest):
    outs, (acc_ref, resid_ref, resid2_ref) = rest[:-3], rest[-3:]
    sources, own, rank, cols = c_ref.shape[0], c_ref.shape[2], c_ref.shape[3], c_ref.shape[4]
    acc_ref[...] = -seen_ref[0, 0].astype(jnp.float32)
    per = max(1, GROUP // own)

    @pl.loop(0, sources // per)
    def _(step):
        first = step * per
        coeff = c_ref[pl.ds(first, per), 0].reshape(per * own * rank, cols)
        acc_ref[...] += dot_rows(part_of(u_ref, (0, 0), first * own, per * own, 0), coeff) + dot_rows(
            part_of(u_ref, (0, 0), first * own, per * own, 1), turn(coeff)
        )

    resid = acc_ref[...].astype(jnp.bfloat16)
    resid_ref[...] = resid
    resid2_ref[...] = turn_back(resid)

    @pl.loop(0, sources // per)
    def _(step):
        first = step * per
        total = dot(part_of(u_ref, (0, 0), first * own, per * own, 0), resid_ref[...])
        total += dot(part_of(u_ref, (0, 0), first * own, per * own, 1), resid2_ref[...])
        back = total.astype(jnp.bfloat16).reshape(per, own, rank, cols)
        for d in range(per):
            for j in range(own):
                outs[j][first + d, 0] = back[d, j]


def middle_call(freq, u_factor, arrived, seen):
    _, own, tiles, _, rank, width = u_factor.shape
    sources = tiles // own
    cols = seen.shape[-1]
    return pl.pallas_call(
        middle_body,
        grid=(own,),
        in_specs=[
            pl.BlockSpec((1, 1, tiles, 2, rank, width), lambda i: (freq, i, 0, 0, 0, 0)),
            pl.BlockSpec((sources, 1, own, rank, cols), lambda i: (0, i, 0, 0, 0)),
            pl.BlockSpec((1, 1, width, cols), lambda i: (freq, i, 0, 0)),
        ],
        out_specs=[pl.BlockSpec((sources, 1, rank, cols), lambda i: (0, i, 0, 0))] * own,
        out_shape=[jax.ShapeDtypeStruct((sources, own, rank, cols), jnp.bfloat16)] * own,
        scratch_shapes=[
            pltpu.VMEM((width, cols), jnp.float32),
            pltpu.VMEM((width, cols), jnp.bfloat16),
            pltpu.VMEM((width, cols), jnp.bfloat16),
        ],
        compiler_params=pltpu.CompilerParams(vmem_limit_bytes=VMEM_BYTES),
        cost_estimate=pl.CostEstimate(
            flops=8 * own * tiles * rank * width * cols,
            bytes_accessed=own * tiles * rank * (4 * width + 4 * cols),
            transcendentals=0,
        ),
        name="middle",
    )(u_factor, arrived.reshape(sources, own, own, rank, cols), seen)


def grad_body(block, freqs, rows_ref, rank_ref, cos_ref, sin_ref, v_ref, *rest):
    backs, out_ref, acc_ref = rest[:freqs], rest[freqs], rest[freqs + 1]
    freq = pl.program_id(0)
    tiles, rank = v_ref.shape[2], v_ref.shape[4]
    cols = acc_ref.shape[1]
    half = cols // 2
    group = min(GROUP, tiles)
    row = lax.broadcasted_iota(jnp.int32, (rank, cols), 0)
    for f in range(freqs):

        @pl.when(freq == f)
        def _():
            acc_ref[f] = jnp.zeros(acc_ref.shape[1:], jnp.float32)

            @pl.loop(0, tiles // group)
            def _(step):
                first = step * group
                picked = []
                for t in range(group):
                    slot = first + t
                    kept = row < rank_ref[f, block, slot]
                    tile = backs[f][rows_ref[block, slot]]
                    picked.append(jnp.where(kept, tile, jnp.zeros_like(tile)))
                back = jnp.concatenate(picked, 0)
                acc_ref[f] += dot_rows(back, part_of(v_ref, (0, 0), first, group, 0)) + dot_rows(
                    turn_back(back), part_of(v_ref, (0, 0), first, group, 1)
                )

    @pl.when(freq == freqs - 1)
    def _():
        chunk = 16
        pairs = out_ref.shape[1]

        @pl.loop(0, half // chunk)
        def _(step):
            here = pl.ds(step * chunk, chunk)
            real = [acc_ref[f, here] for f in range(freqs)]
            imag = [acc_ref[f, pl.ds(half + step * chunk, chunk)] for f in range(freqs)]
            for lag in range(cos_ref.shape[0]):
                total = real[0] * cos_ref[lag, 0] - imag[0] * sin_ref[lag, 0]
                for f in range(1, freqs):
                    total += real[f] * cos_ref[lag, f] - imag[f] * sin_ref[lag, f]
                out_ref[lag // pairs, lag % pairs, here] = total.astype(out_ref.dtype)


def grad_call(block, tile_rows, tile_rank, cosine, sine, v_factor, backs, groups):
    freqs, own, tiles, _, rank, width = v_factor.shape
    cols = backs[0].shape[-1]
    lags = cosine.shape[0]
    whole = pl.BlockSpec((tiles, rank, cols), lambda f, *_: (0, 0, 0))
    return pl.pallas_call(
        functools.partial(grad_body, block, freqs),
        grid_spec=pltpu.PrefetchScalarGridSpec(
            num_scalar_prefetch=4,
            grid=(freqs,),
            in_specs=[
                pl.BlockSpec((1, 1, tiles, 2, rank, width), lambda f, *_: (f, block, 0, 0, 0, 0)),
                *[whole] * freqs,
            ],
            out_specs=pl.BlockSpec((groups, lags // groups, cols // 2, width), lambda f, *_: (0, 0, 0, 0)),
            scratch_shapes=[pltpu.VMEM((freqs, cols, width), jnp.float32)],
        ),
        out_shape=jax.ShapeDtypeStruct((groups, lags // groups, cols // 2, width), jnp.bfloat16),
        compiler_params=pltpu.CompilerParams(vmem_limit_bytes=VMEM_BYTES),
        cost_estimate=pl.CostEstimate(
            flops=4 * freqs * tiles * rank * width * cols,
            bytes_accessed=freqs * tiles * rank * (4 * width + 2 * cols),
            transcendentals=0,
        ),
        name="grad",
    )(tile_rows, tile_rank, cosine, sine, v_factor, *backs)


def exchange(array, axis):
    return lax.all_to_all(array, axis, split_axis=0, concat_axis=0, tiled=True)


def per_device(model_freq, recorded, v_factor, u_factor, tile_rank, tile_rows, omega):
    freqs, own, tiles, _, rank, width = v_factor.shape
    cols = model_freq.shape[-1]
    groups = lax.axis_size("freq")
    blocks = model_freq.reshape(freqs, own, width, cols)
    seen = recorded.reshape(freqs, own, width, cols)
    total = freqs * groups
    phase = jnp.arange(total, dtype=jnp.float32)[:, None] * omega[None, :]
    cosine = jnp.cos(phase) * (2.0 / total)
    sine = jnp.sin(phase) * (2.0 / total)

    arrived = []
    for f in range(freqs):
        arrived.append(exchange(coeff_call(f, tile_rows, tile_rank, v_factor, blocks), "tile"))
    backs = [middle_call(f, u_factor, arrived[f], seen) for f in range(freqs)]
    parts = []
    for j in range(own):
        returned = [
            exchange(backs[f][j].reshape(tiles, rank, cols), "tile").reshape(tiles, rank, cols) for f in range(freqs)
        ]
        shares = grad_call(j, tile_rows, tile_rank, cosine, sine, v_factor, returned, groups)
        parts.append(jnp.sum(exchange(shares, "freq").astype(jnp.float32), 0))
    return jnp.swapaxes(jnp.concatenate(parts, 2), 1, 2)


def solution(mesh):
    placed = (
        P("freq", "tile", None),
        P("freq", "tile", None),
        P("freq", "tile", None, None, None, None),
        P("freq", "tile", None, None, None, None),
        P("freq", "tile", None),
        P("tile", None),
        P("freq"),
    )
    return jax.shard_map(
        per_device, mesh=mesh, in_specs=placed, out_specs=P("freq", "tile", None), check_vma=False
    )
```

```python
import functools

import jax
import jax.numpy as jnp
from jax import lax
from jax.experimental import pallas as pl
from jax.experimental.pallas import tpu as pltpu
from jax.sharding import PartitionSpec as P

VMEM_BYTES = 44 * 1024 * 1024
GROUP = 8


def turn(block):
    half = block.shape[-1] // 2
    return jnp.concatenate([-block[:, half:], block[:, :half]], -1)


def turn_back(block):
    half = block.shape[-1] // 2
    return jnp.concatenate([block[:, half:], -block[:, :half]], -1)


def dot(left, right):
    return lax.dot_general(left, right, (((1,), (0,)), ((), ())), preferred_element_type=jnp.float32)


def dot_rows(left, right):
    return lax.dot_general(left, right, (((0,), (0,)), ((), ())), preferred_element_type=jnp.float32)


def part_of(ref, lead, start, count, part):
    rank, width = ref.shape[-2], ref.shape[-1]
    return ref[(*lead, pl.ds(start, count), part)].reshape(count * rank, width)


def coeff_body(freq, rows_ref, rank_ref, v_ref, x_ref, out_ref, x2_ref):
    block = pl.program_id(0)
    tiles, rank, cols = v_ref.shape[2], v_ref.shape[4], x_ref.shape[-1]
    group = min(GROUP, tiles)
    x2_ref[...] = turn(x_ref[0, 0])
    row = lax.broadcasted_iota(jnp.int32, (rank, cols), 0)

    @pl.loop(0, tiles // group)
    def _(step):
        first = step * group
        total = dot(part_of(v_ref, (0, 0), first, group, 0), x_ref[0, 0])
        total += dot(part_of(v_ref, (0, 0), first, group, 1), x2_ref[...])
        for t in range(group):
            slot = first + t
            kept = row < rank_ref[freq, block, slot]
            tile = jnp.where(kept, total[t * rank : (t + 1) * rank], 0.0)
            out_ref[rows_ref[block, slot], 0] = tile.astype(out_ref.dtype)


def coeff_call(freq, tile_rows, tile_rank, v_factor, blocks):
    _, own, tiles, _, rank, width = v_factor.shape
    cols = blocks.shape[-1]
    return pl.pallas_call(
        functools.partial(coeff_body, freq),
        grid_spec=pltpu.PrefetchScalarGridSpec(
            num_scalar_prefetch=2,
            grid=(own,),
            in_specs=[
                pl.BlockSpec((1, 1, tiles, 2, rank, width), lambda j, *_: (freq, j, 0, 0, 0, 0)),
                pl.BlockSpec((1, 1, width, cols), lambda j, *_: (freq, j, 0, 0)),
            ],
            out_specs=pl.BlockSpec((tiles, 1, rank, cols), lambda j, *_: (0, j, 0, 0)),
            scratch_shapes=[pltpu.VMEM((width, cols), jnp.bfloat16)],
        ),
        out_shape=jax.ShapeDtypeStruct((tiles, own, rank, cols), jnp.bfloat16),
        compiler_params=pltpu.CompilerParams(vmem_limit_bytes=VMEM_BYTES),
        cost_estimate=pl.CostEstimate(
            flops=4 * own * tiles * rank * width * cols,
            bytes_accessed=own * tiles * rank * (4 * width + 2 * cols),
            transcendentals=0,
        ),
        name="coeff",
    )(tile_rows, tile_rank, v_factor, blocks)


def cuts_of(own):
    return 2 if own % 2 == 0 else 1


def middle_body(u_ref, c_ref, seen_ref, *rest):
    outs, (acc_ref, resid_ref, resid2_ref) = rest[:-3], rest[-3:]
    sources, own, rank, cols = c_ref.shape[0], c_ref.shape[2], c_ref.shape[3], c_ref.shape[4]
    acc_ref[...] = -seen_ref[0, 0].astype(jnp.float32)
    per = max(1, GROUP // own)

    @pl.loop(0, sources // per)
    def _(step):
        first = step * per
        coeff = c_ref[pl.ds(first, per), 0].reshape(per * own * rank, cols)
        acc_ref[...] += dot_rows(part_of(u_ref, (0, 0), first * own, per * own, 0), coeff) + dot_rows(
            part_of(u_ref, (0, 0), first * own, per * own, 1), turn(coeff)
        )

    resid = acc_ref[...].astype(jnp.bfloat16)
    resid_ref[...] = resid
    resid2_ref[...] = turn_back(resid)

    @pl.loop(0, sources // per)
    def _(step):
        first = step * per
        total = dot(part_of(u_ref, (0, 0), first * own, per * own, 0), resid_ref[...])
        total += dot(part_of(u_ref, (0, 0), first * own, per * own, 1), resid2_ref[...])
        back = total.astype(jnp.bfloat16).reshape(per, own, rank, cols)
        each = own // len(outs)
        for d in range(per):
            for j in range(own):
                outs[j // each][first + d, 0, j % each] = back[d, j]


def middle_call(freq, u_factor, arrived, seen):
    _, own, tiles, _, rank, width = u_factor.shape
    sources = tiles // own
    cols = seen.shape[-1]
    cuts = cuts_of(own)
    each = own // cuts
    return pl.pallas_call(
        middle_body,
        grid=(own,),
        in_specs=[
            pl.BlockSpec((1, 1, tiles, 2, rank, width), lambda i: (freq, i, 0, 0, 0, 0)),
            pl.BlockSpec((sources, 1, own, rank, cols), lambda i: (0, i, 0, 0, 0)),
            pl.BlockSpec((1, 1, width, cols), lambda i: (freq, i, 0, 0)),
        ],
        out_specs=[pl.BlockSpec((sources, 1, each, rank, cols), lambda i: (0, i, 0, 0, 0))] * cuts,
        out_shape=[jax.ShapeDtypeStruct((sources, own, each, rank, cols), jnp.bfloat16)] * cuts,
        scratch_shapes=[
            pltpu.VMEM((width, cols), jnp.float32),
            pltpu.VMEM((width, cols), jnp.bfloat16),
            pltpu.VMEM((width, cols), jnp.bfloat16),
        ],
        compiler_params=pltpu.CompilerParams(vmem_limit_bytes=VMEM_BYTES),
        cost_estimate=pl.CostEstimate(
            flops=8 * own * tiles * rank * width * cols,
            bytes_accessed=own * tiles * rank * (4 * width + 4 * cols),
            transcendentals=0,
        ),
        name="middle",
    )(u_factor, arrived.reshape(sources, own, own, rank, cols), seen)


def grad_body(block, freqs, groups, rows_ref, rank_ref, cos_ref, sin_ref, v_ref, *rest):
    backs, outs, acc_ref = rest[:freqs], rest[-1 - groups : -1], rest[-1]
    freq = pl.program_id(0)
    tiles, rank = v_ref.shape[2], v_ref.shape[4]
    cols = acc_ref.shape[1]
    half = cols // 2
    group = min(GROUP, tiles)
    row = lax.broadcasted_iota(jnp.int32, (rank, cols), 0)
    for f in range(freqs):

        @pl.when(freq == f)
        def _():
            acc_ref[f] = jnp.zeros(acc_ref.shape[1:], jnp.float32)

            @pl.loop(0, tiles // group)
            def _(step):
                first = step * group
                picked = []
                for t in range(group):
                    slot = first + t
                    kept = row < rank_ref[f, block, slot]
                    tile = backs[f][rows_ref[block, slot], 0]
                    picked.append(jnp.where(kept, tile, jnp.zeros_like(tile)))
                back = jnp.concatenate(picked, 0)
                acc_ref[f] += dot_rows(back, part_of(v_ref, (0, 0), first, group, 0)) + dot_rows(
                    turn_back(back), part_of(v_ref, (0, 0), first, group, 1)
                )

    @pl.when(freq == freqs - 1)
    def _():
        chunk = 16
        pairs = outs[0].shape[0]

        @pl.loop(0, half // chunk)
        def _(step):
            here = pl.ds(step * chunk, chunk)
            real = [acc_ref[f, here] for f in range(freqs)]
            imag = [acc_ref[f, pl.ds(half + step * chunk, chunk)] for f in range(freqs)]
            for lag in range(cos_ref.shape[0]):
                total = real[0] * cos_ref[lag, 0] - imag[0] * sin_ref[lag, 0]
                for f in range(1, freqs):
                    total += real[f] * cos_ref[lag, f] - imag[f] * sin_ref[lag, f]
                outs[lag // pairs][lag % pairs, here] = total.astype(jnp.bfloat16)


def grad_call(block, tile_rows, tile_rank, cosine, sine, v_factor, backs, groups, held):
    freqs, own, tiles, _, rank, width = v_factor.shape
    cols = backs[0].shape[-1]
    lags = cosine.shape[0]
    each = backs[0].shape[1]
    whole = pl.BlockSpec((tiles, 1, rank, cols), lambda f, *_: (0, block % each, 0, 0))
    share = (lags // groups, cols // 2, width)
    return pl.pallas_call(
        functools.partial(grad_body, block, freqs, groups),
        grid_spec=pltpu.PrefetchScalarGridSpec(
            num_scalar_prefetch=4,
            grid=(freqs,),
            in_specs=[
                pl.BlockSpec((1, 1, tiles, 2, rank, width), lambda f, *_: (f, block, 0, 0, 0, 0)),
                *[whole] * freqs,
                *[pl.BlockSpec(memory_space=pl.ANY)] * len(held),
            ],
            out_specs=[
                *[pl.BlockSpec(memory_space=pl.ANY)] * len(held),
                *[pl.BlockSpec(share, lambda f, *_: (0, 0, 0))] * groups,
            ],
            scratch_shapes=[pltpu.VMEM((freqs, cols, width), jnp.float32)],
        ),
        out_shape=[
            *[jax.ShapeDtypeStruct(one.shape, one.dtype) for one in held],
            *[jax.ShapeDtypeStruct(share, jnp.bfloat16)] * groups,
        ],
        input_output_aliases={5 + freqs + n: n for n in range(len(held))},
        compiler_params=pltpu.CompilerParams(vmem_limit_bytes=VMEM_BYTES),
        cost_estimate=pl.CostEstimate(
            flops=4 * freqs * tiles * rank * width * cols,
            bytes_accessed=freqs * tiles * rank * (4 * width + 2 * cols),
            transcendentals=0,
        ),
        name="grad",
    )(tile_rows, tile_rank, cosine, sine, v_factor, *backs, *held)


def exchange(array, axis):
    return lax.all_to_all(array, axis, split_axis=0, concat_axis=0, tiled=True)


def per_device(model_freq, recorded, v_factor, u_factor, tile_rank, tile_rows, omega):
    freqs, own, tiles, _, rank, width = v_factor.shape
    cols = model_freq.shape[-1]
    groups = lax.axis_size("freq")
    blocks = model_freq.reshape(freqs, own, width, cols)
    seen = recorded.reshape(freqs, own, width, cols)
    total = freqs * groups
    group = lax.axis_index("freq")
    lag = (jnp.arange(total, dtype=jnp.int32) + group * (total // groups)) % total
    phase = lag.astype(jnp.float32)[:, None] * omega[None, :]
    cosine = jnp.cos(phase) * (2.0 / total)
    sine = jnp.sin(phase) * (2.0 / total)

    arrived = []
    for f in range(freqs):
        arrived.append(exchange(coeff_call(f, tile_rows, tile_rank, v_factor, blocks), "tile"))
    backs = [list(middle_call(f, u_factor, arrived[f], seen)) for f in range(freqs)]
    parts = []
    each = own // cuts_of(own)
    for cut in range(cuts_of(own)):
        returned = [
            exchange(backs[f][cut].reshape(tiles, each, rank, cols), "tile") for f in range(freqs)
        ]
        for j in range(cut * each, (cut + 1) * each):
            held = [backs[-1][cut + 1]] if cut + 1 < cuts_of(own) else []
            shares = grad_call(j, tile_rows, tile_rank, cosine, sine, v_factor, returned, groups, held)
            if held:
                backs[-1][cut + 1] = shares[0]
                shares = shares[1:]
            summed = shares[0].astype(jnp.float32)
            for d in range(1, groups):
                step = [(z, (z + d) % groups) for z in range(groups)]
                summed += lax.ppermute(shares[d], "freq", step).astype(jnp.float32)
            parts.append(summed)
    return jnp.swapaxes(jnp.concatenate(parts, 2), 1, 2)


def solution(mesh):
    placed = (
        P("freq", "tile", None),
        P("freq", "tile", None),
        P("freq", "tile", None, None, None, None),
        P("freq", "tile", None, None, None, None),
        P("freq", "tile", None),
        P("tile", None),
        P("freq"),
    )
    return jax.shard_map(
        per_device, mesh=mesh, in_specs=placed, out_specs=P("freq", "tile", None), check_vma=False
    )
```
